32 devices in a mesh: dp: 8 (over y, x, core), feat: 4 (over z).
Axes of the slice: x: 2, y: 2, z: 4, core: 2. Of those that a mesh axis runs over, the one named last changes fastest.
Arguments:
- tokens: bfloat16 [4096, 16384], P('dp', 'feat'), may hold values from -6 to 6
- weight: bfloat16 [32, 6, 512, 512], P('feat'), may hold values from -0.15625 to 0.15625
- cotangent: bfloat16 [4096, 16384], P('dp', 'feat'), may hold values from -6 to 6
Outputs:
- output: bfloat16 [4096, 16384], P('dp', 'feat')
- input_grad: bfloat16 [4096, 16384], P('dp', 'feat')
- weight_grad: float32 [32, 6, 512, 512], P('feat', None, 'dp')
The draws below stay inside these ranges and needn't reach their ends.
All inputs are finite; a program needn't handle non-finite values.
Results may differ from the reference program's by a relative error of at most 0.0057.
Values may be sent and summed in bfloat16 or wider, within the bound.
No kernel may reach another device: no remote copies, remote signals or barrier semaphores. Data moves between devices by JAX's collectives and lax.ppermute only.
A program may use at most 256 MiB of HBM per device.

```python
from functools import partial
import jax
import jax.numpy as jnp
import numpy as np

BLK = 512
NB = 32
PARTNERS = 6
D = 16384
TOKENS = 4096


def levels(key, extent, split, least, largest):
    loudness, own = 1.0, jax.random.fold_in(key, 6)
    for dim, parts in split:
        steps = jnp.exp(jax.random.uniform(jax.random.fold_in(own, dim), (parts,), jnp.float32, least / len(split), largest / len(split)))
        loudness = loudness * jnp.repeat(steps, extent[dim] // parts).reshape([-1 if axis == dim else 1 for axis in range(len(extent))])
    return loudness


def centred(stream_key, extent, scale, limit, split=(), dtype=jnp.bfloat16):
    level = levels(stream_key, extent, split, -0.22, 0.18) if split else 1.0
    array = jax.random.normal(stream_key, extent, jnp.float32) * scale * level
    return jnp.minimum(jnp.maximum(array, -limit), limit).astype(dtype)


def setup_inputs(seed: int = 0) -> dict:
    splits = jax.random.split(jax.random.key(seed), 4)
    tokens = centred(splits[0], (TOKENS, D), 1.0, 6.0, ((0, 8), (1, 4)))
    weight = centred(splits[1], (NB, PARTNERS, BLK, BLK), (PARTNERS * BLK // 2) ** -0.5, 0.15625, ((0, 4),))
    cotangent = centred(splits[2], (TOKENS, D), 1.0, 6.0, ((0, 8), (1, 4)))
    return {"tokens": tokens, "weight": weight, "cotangent": cotangent}


gelu_tanh = partial(jax.nn.gelu, approximate=True)

def partner_order(which):
    if which == 0:
        return np.arange(NB)
    return np.arange(NB) ^ 1 << which - 1

def mix_layer(blocks, weight):
    total = jnp.zeros((blocks.shape[0], NB, BLK), jnp.float32)
    for which in range(PARTNERS):
        moved = blocks[:, partner_order(which), :].astype(jnp.float32)
        total = total + jnp.einsum('tnb,nbc->tnc', moved, weight[:, which].astype(jnp.float32))
    return total

def weight_grads(blocks, delta):
    stacked = []
    for which in range(PARTNERS):
        moved = blocks[:, partner_order(which), :].astype(jnp.float32)
        stacked.append(jnp.einsum('tnb,tnc->nbc', moved, delta.astype(jnp.float32)))
    return jnp.stack(stacked, axis=1)

def back_sum(delta, weight):
    total = jnp.zeros(delta.shape, jnp.float32)
    for which in range(PARTNERS):
        term = jnp.einsum('tnc,nbc->tnb', delta.astype(jnp.float32), weight[:, which].astype(jnp.float32))
        term = term.astype(jnp.bfloat16)
        total = total + term[:, partner_order(which), :].astype(jnp.float32)
    return total

def reference(tokens, weight, cotangent):
    inputs = tokens.reshape(TOKENS, NB, BLK)
    z_value = mix_layer(inputs, weight)
    output = gelu_tanh(z_value).astype(jnp.bfloat16)
    unused, pull_back = jax.vjp(gelu_tanh, z_value)
    delta = pull_back(cotangent.reshape(TOKENS, NB, BLK).astype(jnp.float32))[0].astype(jnp.bfloat16)
    weight_grad = weight_grads(inputs, delta)
    input_grad = back_sum(delta, weight).astype(jnp.bfloat16)
    return (output.reshape(TOKENS, D), input_grad.reshape(TOKENS, D), weight_grad)
```

```python
from functools import partial

import jax
import jax.numpy as jnp
from jax import lax
from jax.experimental import pallas as pl
from jax.experimental.pallas import tpu as pltpu
from jax.sharding import PartitionSpec as P

VMEM_BYTES = 48 * 2**20
GELU_SCALE = 0.7978845608028654
GELU_CUBIC = 0.044715

any_spec = pl.BlockSpec(memory_space=pl.ANY)


def dot(left, right, contract):
    return lax.dot_general(left, right, (contract, ((), ())), preferred_element_type=jnp.float32)


def gelu_and_slope(value):
    square = value * value
    tanh = jnp.tanh(GELU_SCALE * (value + GELU_CUBIC * (square * value)))
    half = 0.5 * (1.0 + tanh)
    inner = GELU_SCALE * (1.0 + (3.0 * GELU_CUBIC) * square)
    return value * half, half + 0.5 * value * (1.0 - tanh * tanh) * inner


def swapped(value, level):
    mask = 1 << level
    pairs = [(source, source ^ mask) for source in range(lax.axis_size("feat"))]
    return lax.ppermute(value, "feat", pairs)


def block_step(partners, near, split, *refs):
    far = partners - near
    parts = refs[:partners]
    weight, cotangent = refs[partners : partners + 2]
    output, delta_out, grads = refs[-3 - far : -far] if far else refs[-3:]
    terms = refs[-far:] if far else ()
    total = dot(parts[0][...], weight[0, 0], ((1,), (0,)))
    for which in range(1, partners):
        total = total + dot(parts[which][...], weight[0, which], ((1,), (0,)))
    value, slope = gelu_and_slope(total)
    output[...] = value.astype(output.dtype)
    delta = (cotangent[...].astype(jnp.float32) * slope).astype(delta_out.dtype)
    delta_out[...] = delta
    for index in range(far):
        terms[index][...] = dot(delta, weight[0, near + index], ((1,), (1,))).astype(delta.dtype)
    for which in range(partners):
        grad = dot(parts[which][...], delta, ((0,), (0,))).astype(grads.dtype)
        grads[:, 0, which] = grad.reshape(split, grad.shape[0] // split, grad.shape[1])


def near_step(near, *refs):
    deltas, weights, total = refs[:near], refs[near : 2 * near], refs[-1]
    value = dot(deltas[0][...], weights[0][0, 0], ((1,), (1,)))
    for which in range(1, near):
        value = value + dot(deltas[which][...], weights[which][0, 0], ((1,), (1,)))
    total[...] = value


def last_step(far, *refs):
    value = refs[0][...]
    for index in range(far):
        value = value + refs[1 + index][...].astype(jnp.float32)
    refs[-1][...] = value.astype(refs[-1].dtype)


def local(tokens, weight, cotangent):
    rows = tokens.shape[0]
    blocks, partners, width = weight.shape[:3]
    near = blocks.bit_length()
    far = partners - near
    split = lax.axis_size("dp")
    shard = width // split
    sixteen = tokens.dtype
    params = pltpu.CompilerParams(vmem_limit_bytes=VMEM_BYTES)

    def column(index):
        return pl.BlockSpec((rows, width), lambda *_: (0, index))

    groups, first = [], 0
    while first < blocks:
        size = max(first, 1)
        groups.append((first, size))
        first += size

    arrived = []
    for index, (first, size) in enumerate(groups):
        piece = tokens[:, first * width : (first + size) * width]
        if index >= 3:
            piece, arrived[index - 3] = lax.optimization_barrier((piece, arrived[index - 3]))
        arrived.append([swapped(piece, level) for level in reversed(range(far))][::-1])

    halves = 2 if blocks > 1 else 1
    per_half = blocks // halves
    output = delta = None
    received, scattered = [], []
    for (first, size), pieces in zip(groups, arrived):
        for block in range(first, first + size):
            if block % per_half == 0:
                grads = None
            at = block % per_half
            parts = [tokens] + [tokens] * (near - 1) + list(pieces)
            specs = [column(block)] + [column(block ^ (1 << bit)) for bit in range(near - 1)]
            specs += [column(block - first)] * far
            operands = parts + [weight, cotangent]
            specs += [
                pl.BlockSpec((1, partners, width, width), lambda *_, block=block: (block, 0, 0, 0)),
                column(block),
            ]
            aliases = {}
            for where, chained in enumerate((output, delta, grads)):
                if chained is not None:
                    aliases[len(operands)] = where
                    operands.append(chained)
                    specs.append(any_spec)
            moved = 2 * (3 * partners * width * width + rows * width * (partners + far + 3))
            output, delta, grads, *terms = pl.pallas_call(
                partial(block_step, partners, near, split),
                grid=(1,),
                in_specs=specs,
                out_specs=[
                    column(block),
                    column(block),
                    pl.BlockSpec((split, 1, partners, shard, width), lambda *_, at=at: (0, at, 0, 0, 0)),
                ]
                + [column(0)] * far,
                out_shape=[
                    jax.ShapeDtypeStruct(tokens.shape, sixteen),
                    jax.ShapeDtypeStruct(tokens.shape, sixteen),
                    jax.ShapeDtypeStruct((split, per_half, partners, shard, width), sixteen),
                ]
                + [jax.ShapeDtypeStruct((rows, width), sixteen)] * far,
                input_output_aliases=aliases,
                compiler_params=params,
                cost_estimate=pl.CostEstimate(
                    flops=2 * rows * width * width * (2 * partners + far),
                    bytes_accessed=moved,
                    transcendentals=rows * width,
                ),
                name="block_step",
            )(*operands)
            received.append([swapped(terms[level], level) for level in reversed(range(far))][::-1])
            if at == per_half - 1:
                scattered.append(lax.psum_scatter(grads, "dp", scatter_dimension=0, tiled=False))

    near_total = pl.pallas_call(
        partial(near_step, near),
        grid=(blocks,),
        in_specs=[
            pl.BlockSpec((rows, width), lambda m, mask=mask: (0, m ^ mask))
            for mask in [0] + [1 << bit for bit in range(near - 1)]
        ]
        + [
            pl.BlockSpec((1, 1, width, width), lambda m, mask=mask, which=which: (m ^ mask, which, 0, 0))
            for which, mask in enumerate([0] + [1 << bit for bit in range(near - 1)])
        ],
        out_specs=pl.BlockSpec((rows, width), lambda m: (0, m)),
        out_shape=jax.ShapeDtypeStruct(tokens.shape, jnp.float32),
        compiler_params=params,
        cost_estimate=pl.CostEstimate(
            flops=2 * rows * width * width * near * blocks,
            bytes_accessed=blocks * near * 2 * width * (rows + width) + 4 * rows * width * blocks,
            transcendentals=0,
        ),
        name="near_step",
    )(*[delta] * near, *[weight] * near)

    input_grad = None
    for block in range(blocks):
        operands = [near_total] + received[block]
        specs = [column(block)] + [column(0)] * far
        aliases = {}
        if input_grad is not None:
            aliases[len(operands)] = 0
            operands.append(input_grad)
            specs.append(any_spec)
        input_grad = pl.pallas_call(
            partial(last_step, far),
            grid=(1,),
            in_specs=specs,
            out_specs=column(block),
            out_shape=jax.ShapeDtypeStruct(tokens.shape, sixteen),
            input_output_aliases=aliases,
            compiler_params=params,
            cost_estimate=pl.CostEstimate(
                flops=rows * width * far, bytes_accessed=rows * width * (6 + 2 * far), transcendentals=0
            ),
            name="last_step",
        )(*operands)

    weight_grad = jnp.concatenate(scattered, axis=0).astype(jnp.float32)
    return output, input_grad, weight_grad


def solution(mesh):
    return jax.shard_map(
        local,
        mesh=mesh,
        in_specs=(P("dp", "feat"), P("feat", None, None, None), P("dp", "feat")),
        out_specs=(P("dp", "feat"), P("dp", "feat"), P("feat", None, "dp", None)),
        check_vma=False,
    )
```

```python
from functools import partial

import jax
import jax.numpy as jnp
from jax import lax
from jax.experimental import pallas as pl
from jax.experimental.pallas import tpu as pltpu
from jax.sharding import PartitionSpec as P

VMEM_BYTES = 48 * 2**20
LAG = 6
WINDOW = 2
TIE = 1
GELU_SCALE = 0.7978845608028654
GELU_CUBIC = 0.044715

any_spec = pl.BlockSpec(memory_space=pl.ANY)


def dot(left, right, contract):
    return lax.dot_general(left, right, (contract, ((), ())), preferred_element_type=jnp.float32)


def gelu_and_slope(value):
    square = value * value
    tanh = jnp.tanh(GELU_SCALE * (value + GELU_CUBIC * (square * value)))
    half = 0.5 * (1.0 + tanh)
    inner = GELU_SCALE * (1.0 + (3.0 * GELU_CUBIC) * square)
    return value * half, half + 0.5 * value * (1.0 - tanh * tanh) * inner


def swapped(value, level):
    mask = 1 << level
    pairs = [(source, source ^ mask) for source in range(lax.axis_size("feat"))]
    return lax.ppermute(value, "feat", pairs)


def block_step(partners, near, split, *refs):
    far = partners - near
    parts = refs[:partners]
    weight, cotangent = refs[partners : partners + 2]
    output, delta_out, grads = refs[-3 - far : -far] if far else refs[-3:]
    terms = refs[-far:] if far else ()
    total = dot(parts[0][...], weight[0, 0], ((1,), (0,)))
    for which in range(1, partners):
        total = total + dot(parts[which][...], weight[0, which], ((1,), (0,)))
    value, slope = gelu_and_slope(total)
    output[...] = value.astype(output.dtype)
    delta = (cotangent[...].astype(jnp.float32) * slope).astype(delta_out.dtype)
    delta_out[...] = delta
    for index in range(far):
        terms[index][...] = dot(delta, weight[0, near + index], ((1,), (1,))).astype(delta.dtype)
    for which in range(partners):
        grad = dot(parts[which][...], delta, ((0,), (0,))).astype(grads.dtype)
        grads[:, 0, which] = grad.reshape(split, grad.shape[0] // split, grad.shape[1])


def near_step(near, *refs):
    deltas, weights, total = refs[:near], refs[near : 2 * near], refs[-1]
    value = dot(deltas[0][...], weights[0][0, 0], ((1,), (1,)))
    for which in range(1, near):
        value = value + dot(deltas[which][...], weights[which][0, 0], ((1,), (1,)))
    total[...] = value


def last_step(far, *refs):
    value = refs[0][...]
    for index in range(far):
        value = value + refs[1 + index][...].astype(jnp.float32)
    refs[-1][...] = value.astype(refs[-1].dtype)


def local(tokens, weight, cotangent):
    rows = tokens.shape[0]
    blocks, partners, width = weight.shape[:3]
    near = blocks.bit_length()
    far = partners - near
    split = lax.axis_size("dp")
    shard = width // split
    sixteen = tokens.dtype
    params = pltpu.CompilerParams(vmem_limit_bytes=VMEM_BYTES)

    def column(index):
        return pl.BlockSpec((rows, width), lambda *_: (0, index))

    order = []
    for block in range(blocks):
        order.append((False, block))
        if block >= LAG:
            order.append((True, block - LAG))
    order += [(True, block) for block in range(max(blocks - LAG, 0), blocks)]

    halves = 2 if blocks > 1 else 1
    per_half = blocks // halves
    output = delta = grads = None
    ahead, back, terms, scattered, landed = {}, {}, {}, [], []

    def step(block):
        nonlocal output, delta, grads
        pieces = ahead[block]
        if block >= LAG:
            pieces, back[block - LAG] = lax.optimization_barrier((pieces, back[block - LAG]))
        at = block % per_half
        if at == 0:
            grads = None
        operands = [tokens] * near + pieces + [weight, cotangent]
        specs = [column(block)] + [column(block ^ (1 << bit)) for bit in range(near - 1)]
        specs += [column(0)] * far
        specs += [pl.BlockSpec((1, partners, width, width), lambda *_: (block, 0, 0, 0)), column(block)]
        aliases = {}
        for where, chained in enumerate((output, delta, grads)):
            if chained is not None:
                aliases[len(operands)] = where
                operands.append(chained)
                specs.append(any_spec)
        moved = 2 * (3 * partners * width * width + rows * width * (partners + far + 3))
        output, delta, grads, *terms[block] = pl.pallas_call(
            partial(block_step, partners, near, split),
            grid=(1,),
            in_specs=specs,
            out_specs=[
                column(block),
                column(block),
                pl.BlockSpec((split, 1, partners, shard, width), lambda *_: (0, at, 0, 0, 0)),
            ]
            + [column(0)] * far,
            out_shape=[
                jax.ShapeDtypeStruct(tokens.shape, sixteen),
                jax.ShapeDtypeStruct(tokens.shape, sixteen),
                jax.ShapeDtypeStruct((split, per_half, partners, shard, width), sixteen),
            ]
            + [jax.ShapeDtypeStruct((rows, width), sixteen)] * far,
            input_output_aliases=aliases,
            compiler_params=params,
            cost_estimate=pl.CostEstimate(
                flops=2 * rows * width * width * (2 * partners + far),
                bytes_accessed=moved,
                transcendentals=rows * width,
            ),
            name="block_step",
        )(*operands)
        if at == per_half - 1:
            if TIE:
                waiting.append([order.index((False, block)) + TIE, grads])
            else:
                scattered.append(lax.psum_scatter(grads, "dp", scatter_dimension=0, tiled=False))

    waiting = []
    for place, (backward, block) in enumerate(order):
        if backward:
            step(block)
            pieces = terms[block]
        else:
            pieces = [tokens[:, block * width : (block + 1) * width]] * far
        if place >= WINDOW:
            was, before = order[place - WINDOW]
            held = (back if was else ahead)[before]
            pieces, held = lax.optimization_barrier((pieces, held))
            (back if was else ahead)[before] = held
        sent = [swapped(pieces[level], level) for level in reversed(range(far))][::-1]
        (back if backward else ahead)[block] = sent
    for place, grads in waiting:
        was, before = order[place]
        held = (back if was else ahead)[before]
        grads, held = lax.optimization_barrier((grads, held))
        (back if was else ahead)[before] = held
        scattered.append(lax.psum_scatter(grads, "dp", scatter_dimension=0, tiled=False))

    near_total = pl.pallas_call(
        partial(near_step, near),
        grid=(blocks,),
        in_specs=[
            pl.BlockSpec((rows, width), lambda m, mask=mask: (0, m ^ mask))
            for mask in [0] + [1 << bit for bit in range(near - 1)]
        ]
        + [
            pl.BlockSpec((1, 1, width, width), lambda m, mask=mask, which=which: (m ^ mask, which, 0, 0))
            for which, mask in enumerate([0] + [1 << bit for bit in range(near - 1)])
        ],
        out_specs=pl.BlockSpec((rows, width), lambda m: (0, m)),
        out_shape=jax.ShapeDtypeStruct(tokens.shape, jnp.float32),
        compiler_params=params,
        cost_estimate=pl.CostEstimate(
            flops=2 * rows * width * width * near * blocks,
            bytes_accessed=blocks * near * 2 * width * (rows + width) + 4 * rows * width * blocks,
            transcendentals=0,
        ),
        name="near_step",
    )(*[delta] * near, *[weight] * near)

    weight_grad = jnp.concatenate(scattered, axis=0).astype(jnp.float32)
    input_grad = None
    for block in range(blocks):
        if block == max(blocks - 2, 0):
            weight_grad, back[block] = lax.optimization_barrier((weight_grad, back[block]))
        operands = [near_total] + back[block]
        specs = [column(block)] + [column(0)] * far
        aliases = {}
        if input_grad is not None:
            aliases[len(operands)] = 0
            operands.append(input_grad)
            specs.append(any_spec)
        input_grad = pl.pallas_call(
            partial(last_step, far),
            grid=(1,),
            in_specs=specs,
            out_specs=column(block),
            out_shape=jax.ShapeDtypeStruct(tokens.shape, sixteen),
            input_output_aliases=aliases,
            compiler_params=params,
            cost_estimate=pl.CostEstimate(
                flops=rows * width * far, bytes_accessed=rows * width * (6 + 2 * far), transcendentals=0
            ),
            name="last_step",
        )(*operands)

    return output, input_grad, weight_grad


def solution(mesh):
    return jax.shard_map(
        local,
        mesh=mesh,
        in_specs=(P("dp", "feat"), P("feat", None, None, None), P("dp", "feat")),
        out_specs=(P("dp", "feat"), P("dp", "feat"), P("feat", None, "dp", None)),
        check_vma=False,
    )
```

```python
from functools import partial

import jax
import jax.numpy as jnp
from jax import lax
from jax.experimental import pallas as pl
from jax.experimental.pallas import tpu as pltpu
from jax.sharding import PartitionSpec as P

VMEM_BYTES = 48 * 2**20
LAG = 6
WINDOW = 2
TIE = 1
GELU_SCALE = 0.7978845608028654
GELU_CUBIC = 0.044715

any_spec = pl.BlockSpec(memory_space=pl.ANY)


def dot(left, right, contract):
    return lax.dot_general(left, right, (contract, ((), ())), preferred_element_type=jnp.float32)


def gelu_and_slope(value):
    square = value * value
    tanh = jnp.tanh(GELU_SCALE * (value + GELU_CUBIC * (square * value)))
    half = 0.5 * (1.0 + tanh)
    inner = GELU_SCALE * (1.0 + (3.0 * GELU_CUBIC) * square)
    return value * half, half + 0.5 * value * (1.0 - tanh * tanh) * inner


def swapped(value, level):
    mask = 1 << level
    pairs = [(source, source ^ mask) for source in range(lax.axis_size("feat"))]
    return lax.ppermute(value, "feat", pairs)


def block_step(partners, near, split, *refs):
    far = partners - near
    parts = refs[:partners]
    weight, cotangent = refs[partners : partners + 2]
    output, delta_out, grads = refs[-3 - far : -far] if far else refs[-3:]
    terms = refs[-far:] if far else ()
    total = dot(parts[0][...], weight[0, 0], ((1,), (0,)))
    for which in range(1, partners):
        total = total + dot(parts[which][...], weight[0, which], ((1,), (0,)))
    value, slope = gelu_and_slope(total)
    output[...] = value.astype(output.dtype)
    delta = (cotangent[...].astype(jnp.float32) * slope).astype(delta_out.dtype)
    delta_out[...] = delta
    for index in range(far):
        terms[index][...] = dot(delta, weight[0, near + index], ((1,), (1,))).astype(delta.dtype)
    for which in range(partners):
        grad = dot(parts[which][...], delta, ((0,), (0,))).astype(grads.dtype)
        grads[:, 0, which] = grad.reshape(split, grad.shape[0] // split, grad.shape[1])


def near_step(near, *refs):
    deltas, weights, total = refs[:near], refs[near : 2 * near], refs[-1]
    value = dot(deltas[0][...], weights[0][0, 0], ((1,), (1,)))
    for which in range(1, near):
        value = value + dot(deltas[which][...], weights[which][0, 0], ((1,), (1,)))
    total[...] = value


def last_step(far, *refs):
    value = refs[0][...]
    for index in range(far):
        value = value + refs[1 + index][...].astype(jnp.float32)
    refs[-1][...] = value.astype(refs[-1].dtype)


def local(tokens, weight, cotangent):
    rows = tokens.shape[0]
    blocks, partners, width = weight.shape[:3]
    near = blocks.bit_length()
    far = partners - near
    split = lax.axis_size("dp")
    shard = width // split
    sixteen = tokens.dtype
    params = pltpu.CompilerParams(vmem_limit_bytes=VMEM_BYTES)

    def column(index):
        return pl.BlockSpec((rows, width), lambda *_: (0, index))

    order = []
    for block in range(blocks):
        order.append((False, block))
        if block >= LAG:
            order.append((True, block - LAG))
    order += [(True, block) for block in range(max(blocks - LAG, 0), blocks)]

    halves = 2 if blocks > 1 else 1
    per_half = blocks // halves
    output = delta = grads = None
    ahead, back, terms, scattered, landed = {}, {}, {}, [], []

    def step(block):
        nonlocal output, delta, grads
        pieces = ahead[block]
        if block >= LAG:
            pieces, back[block - LAG] = lax.optimization_barrier((pieces, back[block - LAG]))
        at = block % per_half
        if at == 0:
            grads = None
        operands = [tokens] * near + pieces + [weight, cotangent]
        specs = [column(block)] + [column(block ^ (1 << bit)) for bit in range(near - 1)]
        specs += [column(0)] * far
        specs += [pl.BlockSpec((1, partners, width, width), lambda *_: (block, 0, 0, 0)), column(block)]
        aliases = {}
        for where, chained in enumerate((output, delta, grads)):
            if chained is not None:
                aliases[len(operands)] = where
                operands.append(chained)
                specs.append(any_spec)
        moved = 2 * (3 * partners * width * width + rows * width * (partners + far + 3))
        output, delta, grads, *terms[block] = pl.pallas_call(
            partial(block_step, partners, near, split),
            grid=(1,),
            in_specs=specs,
            out_specs=[
                column(block),
                column(block),
                pl.BlockSpec((split, 1, partners, shard, width), lambda *_: (0, at, 0, 0, 0)),
            ]
            + [column(0)] * far,
            out_shape=[
                jax.ShapeDtypeStruct(tokens.shape, sixteen),
                jax.ShapeDtypeStruct(tokens.shape, sixteen),
                jax.ShapeDtypeStruct((split, per_half, partners, shard, width), sixteen),
            ]
            + [jax.ShapeDtypeStruct((rows, width), sixteen)] * far,
            input_output_aliases=aliases,
            compiler_params=params,
            cost_estimate=pl.CostEstimate(
                flops=int(9 * 1.15e9),
                bytes_accessed=moved,
                transcendentals=rows * width,
            ),
            name="block_step",
        )(*operands)
        if at == per_half - 1:
            if TIE:
                waiting.append([order.index((False, block)) + TIE, grads])
            else:
                scattered.append(lax.psum_scatter(grads, "dp", scatter_dimension=0, tiled=False))

    waiting = []
    for place, (backward, block) in enumerate(order):
        if backward:
            step(block)
            pieces = terms[block]
        else:
            pieces = [tokens[:, block * width : (block + 1) * width]] * far
        if place >= WINDOW:
            was, before = order[place - WINDOW]
            held = (back if was else ahead)[before]
            pieces, held = lax.optimization_barrier((pieces, held))
            (back if was else ahead)[before] = held
        sent = [swapped(pieces[level], level) for level in reversed(range(far))][::-1]
        (back if backward else ahead)[block] = sent
    for place, grads in waiting:
        was, before = order[place]
        held = (back if was else ahead)[before]
        grads, held = lax.optimization_barrier((grads, held))
        (back if was else ahead)[before] = held
        scattered.append(lax.psum_scatter(grads, "dp", scatter_dimension=0, tiled=False))

    near_total = pl.pallas_call(
        partial(near_step, near),
        grid=(blocks,),
        in_specs=[
            pl.BlockSpec((rows, width), lambda m, mask=mask: (0, m ^ mask))
            for mask in [0] + [1 << bit for bit in range(near - 1)]
        ]
        + [
            pl.BlockSpec((1, 1, width, width), lambda m, mask=mask, which=which: (m ^ mask, which, 0, 0))
            for which, mask in enumerate([0] + [1 << bit for bit in range(near - 1)])
        ],
        out_specs=pl.BlockSpec((rows, width), lambda m: (0, m)),
        out_shape=jax.ShapeDtypeStruct(tokens.shape, jnp.float32),
        compiler_params=params,
        cost_estimate=pl.CostEstimate(
            flops=int(200 * 1.15e9),
            bytes_accessed=blocks * near * 2 * width * (rows + width) + 4 * rows * width * blocks,
            transcendentals=0,
        ),
        name="near_step",
    )(*[delta] * near, *[weight] * near)

    weight_grad = jnp.concatenate(scattered, axis=0).astype(jnp.float32)
    input_grad = None
    for block in range(blocks):
        if block == max(blocks - 2, 0):
            weight_grad, back[block] = lax.optimization_barrier((weight_grad, back[block]))
        operands = [near_total] + back[block]
        specs = [column(block)] + [column(0)] * far
        aliases = {}
        if input_grad is not None:
            aliases[len(operands)] = 0
            operands.append(input_grad)
            specs.append(any_spec)
        input_grad = pl.pallas_call(
            partial(last_step, far),
            grid=(1,),
            in_specs=specs,
            out_specs=column(block),
            out_shape=jax.ShapeDtypeStruct(tokens.shape, sixteen),
            input_output_aliases=aliases,
            compiler_params=params,
            cost_estimate=pl.CostEstimate(
                flops=int(25 * 1.15e9), bytes_accessed=rows * width * (6 + 2 * far), transcendentals=0
            ),
            name="last_step",
        )(*operands)

    return output, input_grad, weight_grad


def solution(mesh):
    return jax.shard_map(
        local,
        mesh=mesh,
        in_specs=(P("dp", "feat"), P("feat", None, None, None), P("dp", "feat")),
        out_specs=(P("dp", "feat"), P("dp", "feat"), P("feat", None, "dp", None)),
        check_vma=False,
    )
```
